32 devices in a mesh: row: 8 (over y, x, core), col: 4 (over z).
Axes of the slice: x: 2, y: 2, z: 4, core: 2. Of those that a mesh axis runs over, the one named last changes fastest.
Arguments:
- right_sides: float32 [15, 512, 4096], P(None, 'row', 'col'), may hold values from -6 to 6
- diag_inverse: bfloat16 [15, 4096, 4096], P(None, 'row', 'col'), may hold values from -2 to 2, as said below
- panels: bfloat16 [14, 3, 4096, 4096], P(None, None, 'col', 'row'), may hold values from -0.046875 to 0.046875
- block_map: int32 [14, 4, 3], replicated, may hold values from 8 to 15, as said below
Outputs:
- solution: float32 [15, 512, 4096], P(None, 'col', 'row')
The draws below stay inside these ranges and needn't reach their ends.
Inputs may be any that keep to these rules, and one draw needn't show every extreme that they name: `block_map`: entry [s, q, c] is an ancestor of supernode s, or 15, which marks an empty slot; the ancestors named in one [s, q] are distinct. Each diag_inverse[n] is lower triangular: entries whose column index exceeds the row index are zero.
All inputs are finite; a program needn't handle non-finite values.
Results may differ from the reference program's by a relative error of at most 0.028.
Values may be sent and summed in bfloat16 or wider, within the bound.
A program may use at most 192 MiB of HBM per device.

```python
import math
import jax
import jax.numpy as jnp
import numpy as np
from jax import lax

W = 4096
R = 512
LEV = 4
S = 15
SP = 14
CAP = 3
NBLK = 4
BLK = 1024
SPAN = 512
N_ROW = 8
N_COL = 4


def draw_diag_inverse(key, part):
    first_key = jax.random.fold_in(key, 11)
    second_key = jax.random.fold_in(key, 12)
    spread = jnp.clip(jax.random.normal(first_key, (S, W, W), jnp.float32), -5.0, 5.0)
    pivots = jax.random.uniform(second_key, (S, W), jnp.float32, 0.6, 1.4)
    rows_iota = lax.broadcasted_iota(jnp.int32, (S, W, W), 1)
    cols_iota = lax.broadcasted_iota(jnp.int32, (S, W, W), 2)
    below_part = jnp.where(cols_iota < rows_iota, spread * (0.6 / math.sqrt(W)), 0.0)
    diagonal = jnp.where(cols_iota == rows_iota, pivots[:, :, None], 0.0)
    return (below_part + diagonal).astype(jnp.bfloat16)


def ancestor_table():
    ancestors = np.full((S - 1, LEV - 1), S, np.int32)
    for supernode in range(S - 1):
        level_index = LEV - 1
        while supernode >= 2 ** LEV - 2 ** level_index:
            level_index -= 1
        local_index = supernode - (2 ** LEV - 2 ** (level_index + 1))
        for distance in range(1, level_index + 1):
            ancestors[supernode, distance - 1] = 2 ** LEV - 2 ** (level_index - distance + 1) + (local_index >> distance)
    return ancestors


def draw_block_map(key, part):
    ancestors = jnp.asarray(ancestor_table())
    level_key = jax.random.fold_in(key, 21)
    live_key = jax.random.fold_in(key, 22)
    turn_key = jax.random.fold_in(key, 23)
    thresholds = jax.random.randint(level_key, (1, NBLK, 1), 1, 5)
    rolls = jax.random.randint(live_key, (S - 1, NBLK, LEV - 1), 0, 4)
    entries = jnp.where(rolls < thresholds, ancestors[:, None, :], S)
    turns = jax.random.randint(turn_key, (S - 1, NBLK, 1), 0, LEV - 1)
    order = (lax.broadcasted_iota(jnp.int32, (S - 1, NBLK, LEV - 1), 2) + turns) % (LEV - 1)
    return jnp.take_along_axis(entries, order, axis=2).astype(jnp.int32)


def block_scale(stream_key, shape, cuts, least, high):
    loudness = 1.0
    for dim, blocks in cuts:
        draws = jax.random.uniform(jax.random.fold_in(jax.random.fold_in(stream_key, 6), dim), (blocks,), jnp.float32, least / len(cuts), high / len(cuts))
        loudness = loudness * jnp.repeat(jnp.exp(draws), shape[dim] // blocks).reshape((-1,) + (1,) * (len(shape) - 1 - dim))
    return loudness


def normal_values(rng, extent, scale, reach, cuts=(), kind=jnp.bfloat16):
    gain = block_scale(rng, extent, cuts, -0.22, 0.18) if cuts else 1.0
    values = jax.random.normal(rng, extent, jnp.float32) * scale * gain
    return jnp.minimum(jnp.maximum(values, -reach), reach).astype(kind)


def setup_inputs(seed: int = 0) -> dict:
    seeds = jax.random.split(jax.random.key(seed), 5)
    return {
        "right_sides": normal_values(seeds[0], (S, R, W), 1.0, 6.0, ((1, 8), (2, 4)), jnp.float32),
        "diag_inverse": draw_diag_inverse(jax.random.fold_in(seeds[4], 71), 0),
        "panels": normal_values(seeds[2], (SP, CAP, W, W), (4 * W) ** -0.5, 0.046875, ((2, 4), (3, 8))),
        "block_map": draw_block_map(jax.random.fold_in(seeds[4], 71), 0),
    }


def node_tier(supernode):
    level_index = LEV - 1
    while supernode >= 2 ** LEV - 2 ** level_index:
        level_index -= 1
    return level_index


def ancestor_of(supernode, distance):
    level_index = node_tier(supernode)
    local_index = supernode - (2 ** LEV - 2 ** (level_index + 1))
    return 2 ** LEV - 2 ** (level_index - distance + 1) + (local_index >> distance)


def descendants_of(target):
    found = []
    for source in range(S - 1):
        for distance in range(1, node_tier(source) + 1):
            if ancestor_of(source, distance) == target:
                found.append(source)
    return found


def reference(right_sides, diag_inverse, panels, block_map):
    outputs = []
    rounded = []
    for level_index in range(LEV - 1, -1, -1):
        for supernode in range(2 ** LEV - 2 ** (level_index + 1), 2 ** LEV - 2 ** level_index):
            residual = right_sides[supernode]
            if level_index < LEV - 1:
                partial_value = jnp.zeros((N_ROW, R, W), jnp.float32)
                for source in descendants_of(supernode):
                    chosen = jnp.repeat((block_map[source] == supernode).T, BLK, axis=1)
                    selected = jnp.sum(jnp.where(chosen[:, :, None], panels[source].astype(jnp.float32), 0.0), axis=0)
                    partial_value = partial_value + jnp.einsum(
                        "cpk,ipk->pci",
                        rounded[source].astype(jnp.float32).reshape(R, N_ROW, SPAN),
                        selected.reshape(W, N_ROW, SPAN),
                        precision=lax.Precision.HIGHEST)
                partial_value = lax.optimization_barrier(partial_value.astype(jnp.bfloat16))
                residual = residual - jnp.sum(partial_value.astype(jnp.float32), axis=0)
            leveled = lax.optimization_barrier(residual.astype(jnp.bfloat16)).astype(jnp.float32)
            pieces = jnp.einsum(
                "cqk,iqk->qci",
                leveled.reshape(R, N_COL, BLK),
                diag_inverse[supernode].astype(jnp.float32).reshape(W, N_COL, BLK),
                precision=lax.Precision.HIGHEST)
            pieces = lax.optimization_barrier(pieces.astype(jnp.bfloat16))
            solution = jnp.sum(pieces.astype(jnp.float32), axis=0)
            outputs.append(solution)
            rounded.append(solution.astype(jnp.bfloat16))
    return jnp.stack(outputs)
```

```python
import functools

import jax
import jax.numpy as jnp
import numpy as np
from jax import lax
from jax.experimental import pallas as pl
from jax.experimental.pallas import tpu as pltpu
from jax.sharding import PartitionSpec as P

LEV = 4
S = 15
PARAMS = pltpu.CompilerParams(vmem_limit_bytes=32 * 2**20)
TRANSPOSED = (((1,), (1,)), ((), ()))


def first_of(level):
    return 2**LEV - 2 ** (level + 1)


def ancestor_table():
    table = np.full((S - 1, LEV - 1), -1, np.int32)
    for level in range(1, LEV):
        for j in range(2**level):
            for distance in range(1, level + 1):
                table[first_of(level) + j, distance - 1] = first_of(level - distance) + (j >> distance)
    return table


def inverse_kernel(residual_ref, inverse_ref, piece_ref):
    senders, _, share, depth = residual_ref.shape
    receivers, _, rows, width = piece_ref.shape
    x = residual_ref[...].reshape(senders * share, depth)
    product = lax.dot_general(x, inverse_ref[0], TRANSPOSED, preferred_element_type=jnp.float32)
    piece_ref[...] = product.astype(piece_ref.dtype).reshape(receivers, 1, rows, width)


def apply_inverse(gathered, inverse, level, receivers):
    senders, count, share, depth = gathered.shape
    width = inverse.shape[1]
    samples = senders * share
    first = first_of(level)
    return pl.pallas_call(
        inverse_kernel,
        grid=(count,),
        in_specs=[
            pl.BlockSpec((senders, 1, share, depth), lambda n: (0, n, 0, 0)),
            pl.BlockSpec((1, width, depth), lambda n: (first + n, 0, 0)),
        ],
        out_specs=pl.BlockSpec((receivers, 1, samples // receivers, width), lambda n: (0, n, 0, 0)),
        out_shape=jax.ShapeDtypeStruct((receivers, count, samples // receivers, width), jnp.bfloat16),
        compiler_params=PARAMS,
        cost_estimate=pl.CostEstimate(
            flops=2 * count * samples * depth * width,
            bytes_accessed=2 * count * (samples * depth + width * depth + samples * width),
            transcendentals=0,
        ),
        name="apply_inverse",
    )(gathered, inverse)


def update_kernel(node_of, slots_ref, solved_ref, panel_ref, *rest, has_initial):
    initial_ref = rest[0] if has_initial else None
    part_ref, total = rest[-2], rest[-1]
    a, d = pl.program_id(0), pl.program_id(1)

    @pl.when(d == 0)
    def _():
        total[...] = initial_ref[...].reshape(total.shape) if has_initial else jnp.zeros_like(total)

    @pl.when(slots_ref[node_of(a, d)] >= 0)
    def _():
        senders, _, rows, depth = solved_ref.shape
        x = solved_ref[...].reshape(senders * rows, depth)
        total[...] += lax.dot_general(x, panel_ref[0, 0], TRANSPOSED, preferred_element_type=jnp.float32)

    @pl.when(d == pl.num_programs(1) - 1)
    def _():
        part_ref[...] = total[...].astype(part_ref.dtype).reshape(part_ref.shape)


def add_update(solved, panels, slots, initial, level, target, receivers, dtype):
    senders, count, rows, depth = solved.shape
    width = panels.shape[2]
    samples = senders * rows
    targets = 2**target
    span = count // targets
    first = first_of(level)
    distance = level - target

    def node_of(a, d):
        return (first + a * span + d) * (LEV - 1) + distance - 1

    block = (receivers, 1, samples // receivers, width)
    total_spec = pl.BlockSpec(block, lambda a, d, slots: (0, a, 0, 0))
    in_specs = [
        pl.BlockSpec((senders, 1, rows, depth), lambda a, d, slots: (0, a * span + d, 0, 0)),
        pl.BlockSpec(
            (1, 1, width, depth),
            lambda a, d, slots: (first + a * span + d, jnp.maximum(slots[node_of(a, d)], 0), 0, 0),
        ),
    ]
    operands = [slots, solved, panels]
    if initial is not None:
        in_specs.append(total_spec)
        operands.append(initial)
    return pl.pallas_call(
        functools.partial(update_kernel, node_of, has_initial=initial is not None),
        grid_spec=pltpu.PrefetchScalarGridSpec(
            num_scalar_prefetch=1,
            grid=(targets, span),
            in_specs=in_specs,
            out_specs=total_spec,
            scratch_shapes=[pltpu.VMEM((samples, width), jnp.float32)],
        ),
        out_shape=jax.ShapeDtypeStruct((receivers, targets, samples // receivers, width), dtype),
        compiler_params=PARAMS,
        cost_estimate=pl.CostEstimate(
            flops=2 * count * samples * depth * width,
            bytes_accessed=2 * count * (samples * depth + width * depth) + 4 * targets * samples * width,
            transcendentals=0,
        ),
        name="add_update",
    )(*operands)


def per_device(right_sides, diag_inverse, panels, block_map):
    row_count = lax.axis_size("row")
    col_count = lax.axis_size("col")
    own_blocks = lax.dynamic_slice_in_dim(block_map, lax.axis_index("col"), 1, 1)[:, 0, :]
    named = own_blocks[:, None, :] == jnp.asarray(ancestor_table())[:, :, None]
    slot_ids = jnp.arange(own_blocks.shape[1], dtype=jnp.int32)
    slots = jnp.max(jnp.where(named, slot_ids, -1), axis=2).reshape(-1)
    pending = {}
    received = None
    results = []
    for level in range(LEV - 1, -1, -1):
        first, count = first_of(level), 2**level
        current = right_sides[first : first + count]
        if received is not None:
            current = current - jnp.sum(received.astype(jnp.float32), axis=0)
        gathered = lax.all_gather(current.astype(jnp.bfloat16), "row", axis=0)
        pieces = apply_inverse(gathered, diag_inverse, level, col_count)
        own = lax.psum_scatter(pieces, "col", scatter_dimension=0, tiled=False)
        results.append(own.astype(jnp.float32))
        if level > 0:
            solved = lax.all_gather(own, "col", axis=0)
            parts = add_update(
                solved, panels, slots, pending.get(level - 1), level, level - 1, row_count, jnp.bfloat16
            )
            received = lax.all_to_all(parts, "row", 0, 0, tiled=True)
            if level > 1:
                solved, received = lax.optimization_barrier((solved, received))
            for target in range(level - 2, -1, -1):
                pending[target] = add_update(
                    solved, panels, slots, pending.get(target), level, target, row_count, jnp.float32
                )
    return jnp.concatenate(results, axis=0)


def solution(mesh):
    return jax.shard_map(
        per_device,
        mesh=mesh,
        in_specs=(P(None, "row", "col"), P(None, "row", "col"), P(None, None, "col", "row"), P()),
        out_specs=P(None, "col", "row"),
        check_vma=False,
    )
```
